1024 devices in a mesh: dp: 32 (over x, y_hi), mp: 32 (over z, y_lo, core).
Axes of the slice: x: 8, y: 8 (y_hi: 4, y_lo: 2; y = y_hi * 2 + y_lo), z: 8, core: 2. Of those that a mesh axis runs over, the one named last changes fastest.
Arguments:
- stream: bfloat16 [262144, 1152], P(('dp', 'mp')), may hold values from -6 to 6
- query_key_value: bfloat16 [262144, 3456], P(('dp', 'mp')), may hold values from -9 to 9
- lengths: int32 [1024, 3], P(('dp', 'mp')), may hold values from 1 to 160, 256 in all within a row
- out_weight: bfloat16 [1152, 1152], P('mp', 'dp'), may hold values from -0.1875 to 0.1875
- text_embed: bfloat16 [3072, 1152], P(('dp', 'mp')), may hold values from -6 to 6
- logit_scale: float32 [1], replicated, may hold values from 5 to 20
- logit_bias: float32 [1], replicated, may hold values from -6 to -3
Outputs:
- stream_out: bfloat16 [262144, 1152], P(('dp', 'mp'))
- image_grad: float32 [3072, 1152], P(('dp', 'mp'))
- text_grad: float32 [3072, 1152], P(('dp', 'mp'))
The draws below stay inside these ranges and needn't reach their ends.
Inputs may be any that keep to these rules, and one draw needn't show every extreme that they name: `lengths`: the 3 counts of each pack sum to 256; the largest of each pack is exactly 160.
All inputs are finite; a program needn't handle non-finite values.
Results may differ from the reference program's by a relative error of at most 0.0034.
Values may be sent and summed in bfloat16 or wider, within the bound.
A program may use at most 32 MiB of HBM per device.

```python
import math
import jax
import jax.numpy as jnp
import numpy as np
from jax import lax

D = 1152
HEADS = 16
ROWS = 256
IMGS = 3
MAXP = 160
PACKS = 1024
TOKENS = 262144
IMAGES = 3072


def draw_query_key_value(key, part):
    key = jax.random.fold_in(key, 11)
    first_key = jax.random.fold_in(key, 0)
    return jnp.clip(jax.random.normal(first_key, (TOKENS, 3 * D), jnp.float32), -6.0, 6.0).astype(jnp.bfloat16)


def levels(key, shape, cuts, least, top_value):
    gain = 1.0
    for position, parts in cuts:
        heights = jax.random.uniform(jax.random.fold_in(jax.random.fold_in(key, 6), position), (parts,), jnp.float32, least / len(cuts), top_value / len(cuts))
        gain = gain * jnp.repeat(jnp.exp(heights), shape[position] // parts).reshape((-1,) + (1,) * (len(shape) - 1 - position))
    return gain


def split_up(number_of, total, bound, skew):
    loads = [(1 << 20) // math.isqrt(standing ** skew) + 1 for standing in range(2, number_of + 1)]
    spare, given = total - bound - (number_of - 1), [1] * (number_of - 1)
    while spare > 0:
        free = [i for i in range(number_of - 1) if given[i] < bound]
        mass, left = sum([loads[i] for i in free]), spare
        for i in free:
            extra = min(bound - given[i], max(1, left * loads[i] // mass), spare)
            given[i] = given[i] + extra
            spare = spare - extra
    return np.array([bound] + given)


def uneven(key, amount, total, bound, lean):
    if amount == 2:
        one = jax.random.randint(key, (), max(1, total - bound), min(bound, total - 1) + 1)
        return jnp.stack([one, total - one])
    tallies = jnp.asarray(split_up(amount, total, bound, lean), jnp.int32)
    pairs = (amount - 1) // 2
    source_of, sink = tallies[1:1 + 2 * pairs:2], tallies[2:2 + 2 * pairs:2]
    margin = jnp.minimum(source_of - 1, bound - sink)
    shifted = jax.random.randint(jax.random.fold_in(key, 1), (pairs,), 0, 1 << 20) % (margin + 1)
    tallies = tallies.at[1:1 + 2 * pairs:2].set(source_of - shifted).at[2:2 + 2 * pairs:2].set(sink + shifted)
    return tallies[jax.random.permutation(jax.random.fold_in(key, 2), amount)]


def bell_draw(stream_key, shape, spread, most, cuts=(), held_as=jnp.bfloat16):
    result = jax.random.normal(stream_key, shape, jnp.float32) * spread
    if len(cuts) > 0:
        result = levels(stream_key, shape, cuts, -0.22, 0.18) * result
    return jnp.clip(result, min=-most, max=most).astype(held_as)


def setup_inputs(seed: int = 0) -> dict:
    keys = jax.random.split(jax.random.key(seed), 8)
    return {
        "stream": bell_draw(keys[0], (TOKENS, D), 1.0, 6.0, ((0, 1024),)),
        "query_key_value": draw_query_key_value(jax.random.fold_in(keys[7], 71), 0),
        "lengths": jax.vmap(lambda own: uneven(own, IMGS, ROWS, MAXP, 2))(jax.random.split(keys[2], PACKS)).reshape((PACKS, IMGS)).astype(jnp.int32),
        "out_weight": bell_draw(keys[3], (D, D), D ** -0.5, 0.1875, ((0, 32), (1, 32))),
        "text_embed": bell_draw(keys[4], (IMAGES, D), 1.0, 6.0, ((0, 1024),)),
        "logit_scale": jnp.clip(jnp.exp(jax.random.uniform(keys[5], (1,), jnp.float32, math.log(5.0), math.log(20.0))), 5.0, 20.0),
        "logit_bias": jnp.clip(jax.random.uniform(keys[6], (1,), jnp.float32, -6.0, -3.0), -6.0, -3.0),
    }


def attend_pack(packed, counts):
    row_count = packed.shape[0]
    model_width = packed.shape[1] // 3
    head_size = model_width // HEADS
    queries = packed[:, :model_width].astype(jnp.float32).reshape(row_count, HEADS, head_size)
    key_rows = packed[:, model_width:2 * model_width].astype(jnp.float32).reshape(row_count, HEADS, head_size)
    value_rows = packed[:, 2 * model_width:].astype(jnp.float32).reshape(row_count, HEADS, head_size)
    boundary = jnp.cumsum(counts, dtype=jnp.int32)
    places = jnp.arange(row_count, dtype=jnp.int32)
    segment = lax.optimization_barrier(jnp.sum((places[:, None] >= boundary[None, :-1]).astype(jnp.int32), axis=1))
    same_image = segment[:, None] == segment[None, :]
    scores = jnp.einsum('qhd,khd->hqk', queries, key_rows) / math.sqrt(head_size)
    scores = jnp.where(same_image[None], scores, jnp.float32(-1e+30))
    peaks = lax.optimization_barrier(jnp.max(scores, axis=2, keepdims=True))
    raised = jnp.exp(scores - peaks)
    attention = (raised / lax.optimization_barrier(jnp.sum(raised, axis=2, keepdims=True))).astype(jnp.bfloat16)
    context = jnp.einsum('hqk,khd->qhd', attention.astype(jnp.float32), value_rows)
    context = context.reshape(row_count, model_width).astype(jnp.bfloat16)
    image_slots = jnp.arange(counts.shape[0], dtype=jnp.int32)
    member = (segment[:, None] == image_slots[None, :]).astype(jnp.bfloat16)
    return (context, member)

def unit_rows(values):
    squares = lax.optimization_barrier(jnp.sum(values * values, axis=1, keepdims=True))
    return values / jnp.sqrt(squares + 1e-06)

def reference(stream, query_key_value, lengths, out_weight, text_embed, logit_scale, logit_bias):

    def one_pack(inputs):
        pack_values, pack_stream, pack_counts = inputs
        context, member = attend_pack(pack_values, pack_counts)
        product = jnp.dot(context, out_weight, preferred_element_type=jnp.float32)
        mixed = (product + pack_stream.astype(jnp.float32)).astype(jnp.bfloat16)
        pooled = jnp.dot(member.T, mixed, preferred_element_type=jnp.float32)
        pooled = pooled / pack_counts.astype(jnp.float32)[:, None]
        return (mixed, pooled)
    mixed, pooled = lax.map(one_pack, (query_key_value.reshape(PACKS, ROWS, 3 * D), stream.reshape(PACKS, ROWS, D), lengths))
    image_unit = unit_rows(pooled.reshape(IMAGES, D))
    text_unit = unit_rows(text_embed.astype(jnp.float32))
    scale = logit_scale[0]
    logits = scale * jnp.dot(image_unit, text_unit.T, precision=lax.Precision.HIGHEST) + logit_bias[0]
    numbers = jnp.arange(IMAGES, dtype=jnp.int32)
    labels = jnp.where(numbers[:, None] == numbers[None, :], jnp.float32(1.0), jnp.float32(-1.0))
    coef = -labels * jax.nn.sigmoid(-labels * logits)
    image_grad = scale * jnp.dot(coef, text_unit, precision=lax.Precision.HIGHEST)
    text_grad = scale * jnp.dot(coef.T, image_unit, precision=lax.Precision.HIGHEST)
    return (mixed.reshape(TOKENS, D), image_grad, text_grad)
```

```python
import functools
import math

import jax
import jax.numpy as jnp
from jax import lax
from jax.experimental import pallas as pl
from jax.experimental.pallas import tpu as pltpu
from jax.sharding import PartitionSpec as P

MESH = pl.DeviceIdType.MESH
HEADS = 16
HEAD = 72
SLAB = 80
ROWS = 256
D = 1152
BLK = 36
HIGHEST = lax.Precision.HIGHEST
STEPS = ((1, 0, 0, 1), (-1, 0, 0, -1), (0, 1, 0, 2), (0, -1, 0, -2), (0, 0, 1, 3), (0, 0, -1, -3))
FAR = ((0, 2, 0, 0, 256), (0, -2, 0, 256, 256), (1, 0, 1, 512, 384), (-1, 0, -1, 896, 256))


def place():
    dp, mp = lax.axis_index("dp"), lax.axis_index("mp")
    return dp // 4, 2 * (dp % 4) + (mp // 2) % 2, mp // 4, mp % 2


def device(x, y, z, c):
    return (x * 4 + y // 2, z * 4 + (y % 2) * 2 + c)


def step_from(x, y, z, c, sx, sy, sz):
    return device((x + sx + 8) % 8, (y + sy + 8) % 8, (z + sz + 8) % 8, c)


def send(src, dst, send_sem, recv_sem, to):
    copy = pltpu.make_async_remote_copy(
        src_ref=src, dst_ref=dst, send_sem=send_sem, recv_sem=recv_sem, device_id=to, device_id_type=MESH
    )
    copy.start()
    return copy


def await_bytes(ref, sem):
    pltpu.make_async_copy(ref, ref, sem).wait()


def shift_lanes(value, amount):
    amount = amount % 128
    return value if amount == 0 else pltpu.roll(value, amount, 1)


def split(value):
    high = value.astype(jnp.bfloat16)
    low = (value - high.astype(jnp.float32)).astype(jnp.bfloat16)
    return high, low


def dot32(a, b, dims):
    return lax.dot_general(a, b, (dims, ((), ())), preferred_element_type=jnp.float32)


def kernel(
    lengths, scale_ref, bias_ref, weight, text, qkv_hbm, stream_hbm,
    out, image_grad, text_grad,
    qkv, stream, raw, rows72, packed, arrived, slabs, context,
    texts, images, table_i, table_t,
    part_i, part_x, sent_i, got_i, sent_t, got_t,
    local_sem, raw_s, raw_r, one_s, one_r, two_s, two_r, fwd_s, fwd_r,
    text_s, text_r, img_s, img_r, imf_s, imf_r, mix_s, mix_r, gi_s, gi_r, gt_s, gt_r,
):
    x, y, z, c = place()
    dp, mp = lax.axis_index("dp"), lax.axis_index("mp")
    yh, yl = y // 2, y % 2
    pair = z * 2 + yl
    sibling = device(x, y, z, 1 - c)
    mine = (x + 2 * y + 3 * z) % 8

    load_qkv = pltpu.make_async_copy(qkv_hbm, qkv, local_sem.at[0])
    load_qkv.start()
    load_stream = pltpu.make_async_copy(stream_hbm, stream, local_sem.at[1])
    load_stream.start()

    raw[...] = jnp.zeros(raw.shape, raw.dtype)
    raw[pl.ds(c, 1), 0:BLK, 0:BLK] = weight[...][None]

    barrier = pltpu.get_barrier_semaphore()

    def greet(to):
        pl.semaphore_signal(barrier, inc=1, device_id=to, device_id_type=MESH)

    def source_of(i):
        return device(i % 8, 2 * (i // 8) + c, mine, 1 - yl)

    def target_of(i):
        ty, tz = 2 * ((yh + i // 8) % 4) + 1 - c, (z + i) % 8
        return device((z + 64 - 2 * ty - 3 * tz) % 8, ty, tz, yl)

    def peer_row(i):
        other = (pair + i) % 16
        return (dp, 2 * other + c), other

    def peer_col(i):
        other = (dp + i) % 32
        return (other, mp), other

    greet(sibling)
    lax.fori_loop(0, 32, lambda i, _: (greet(source_of(i)), 0)[1], 0)
    for sx, sy, sz, _ in STEPS:
        greet(step_from(x, y, z, c, sx, sy, sz))
    for sx, sy, sz, _, _ in FAR:
        greet(step_from(x, y, z, c, sx, sy, sz))
    lax.fori_loop(1, 16, lambda i, _: (greet(peer_row(i)[0]), 0)[1], 0)
    lax.fori_loop(1, 32, lambda i, _: (greet(peer_col(i)[0]), 0)[1], 0)
    pl.semaphore_wait(barrier, 1 + 32 + 6 + 4 + 15 + 31)

    copy = send(raw.at[c], raw.at[c], raw_s, raw_r, sibling)
    copy.wait()
    rows72[0:BLK, :] = raw[0, 0:BLK, :].astype(jnp.float32)
    rows72[BLK : 2 * BLK, :] = raw[1, 0:BLK, :].astype(jnp.float32)
    lane = lax.broadcasted_iota(jnp.int32, (24, 128), 1)
    together = rows72[0:24, :]
    for g in (1, 2):
        piece = shift_lanes(rows72[24 * g : 24 * g + 24, :], BLK * g)
        together = jnp.where((lane >= BLK * g) & (lane < BLK * g + BLK), piece, together)
    packed[...] = together.astype(jnp.bfloat16)

    def first(i, _):
        send(packed, arrived.at[dp], one_s, one_r, target_of(i))
        return 0

    lax.fori_loop(0, 32, first, 0)

    texts[pl.ds(dp, 1)] = text[...][None]

    def second(i, _):
        to, _ = peer_col(i)
        send(text, texts.at[dp], text_s, text_r, to)
        return 0

    lax.fori_loop(1, 32, second, 0)

    count0, count1, count2 = lengths[0, 0], lengths[0, 1], lengths[0, 2]

    def segment(shape, dim):
        at = lax.broadcasted_iota(jnp.int32, shape, dim)
        return (at >= count0).astype(jnp.int32) + (at >= count0 + count1).astype(jnp.int32)

    same = segment((ROWS, ROWS), 0) == segment((ROWS, ROWS), 1)
    load_qkv.wait()
    root = 1.0 / math.sqrt(HEAD)
    context[...] = jnp.zeros(context.shape, context.dtype)
    for h in range(HEADS):
        q = qkv[:, HEAD * h : HEAD * (h + 1)]
        k = qkv[:, D + HEAD * h : D + HEAD * (h + 1)]
        v = qkv[:, 2 * D + HEAD * h : 2 * D + HEAD * (h + 1)]
        scores = jnp.where(same, dot32(q, k, ((1,), (1,))) * root, jnp.float32(-1e30))
        raised = jnp.exp(scores - jnp.max(scores, axis=1, keepdims=True))
        total = jnp.sum(raised, axis=1, keepdims=True)
        attention = (raised / total).astype(jnp.bfloat16)
        mixed = dot32(attention, v, ((1,), (0,)))
        context[:, SLAB * h : SLAB * h + HEAD] = mixed.astype(jnp.bfloat16)

    await_bytes(arrived, one_r)
    lane = lax.broadcasted_iota(jnp.int32, (24, 128), 1)
    bands = []
    for g in range(3):
        tiles = [None] * 9
        for d in range(32):
            piece = shift_lanes(arrived[d].astype(jnp.float32), BLK * d - BLK * g)
            for t in range(BLK * d // 128, (BLK * d + BLK - 1) // 128 + 1):
                at = lane + 128 * t
                keep = at >= BLK * d
                tiles[t] = piece if tiles[t] is None else jnp.where(keep, piece, tiles[t])
        bands.append(jnp.concatenate(tiles, axis=1))
    bands.append(jnp.zeros((8, D), jnp.float32))
    own = 2 * mine + c
    slabs[pl.ds(own, 1)] = jnp.concatenate(bands, axis=0).astype(jnp.bfloat16)[None]

    copies = []
    for i, (sx, sy, sz, _) in enumerate(STEPS):
        to = step_from(x, y, z, c, sx, sy, sz)
        copies.append(send(slabs.at[own], slabs.at[own], two_s.at[i], two_r.at[i], to))
    for i, (sx, sy, sz, start, size) in enumerate(FAR):
        to = step_from(x, y, z, c, sx, sy, sz)
        part = slabs.at[own, :, pl.ds(start, size)]
        copies.append(send(part, part, two_s.at[6 + i], two_r.at[6 + i], to))
    forwards = [send(slabs.at[own], slabs.at[own], fwd_s.at[0], fwd_r.at[0], sibling)]
    for i, (_, _, _, label) in enumerate(STEPS):
        copies[i].wait_recv()
        at = 2 * ((mine - label + 8) % 8) + c
        forwards.append(send(slabs.at[at], slabs.at[at], fwd_s.at[1 + i], fwd_r.at[1 + i], sibling))
    for i in range(6, 10):
        copies[i].wait_recv()
    at = 2 * ((mine + 4) % 8) + c
    forwards.append(send(slabs.at[at], slabs.at[at], fwd_s.at[7], fwd_r.at[7], sibling))
    for copy in forwards:
        copy.wait_recv()

    load_stream.wait()
    numbers = lax.broadcasted_iota(jnp.int32, (8, ROWS), 0)
    member = (segment((8, ROWS), 1) == numbers).astype(jnp.bfloat16)
    row = lax.broadcasted_iota(jnp.int32, (8, 1), 0)
    counts = jnp.where(row == 0, count0, jnp.where(row == 1, count1, count2)).astype(jnp.float32)
    left = context[...]
    pooled = []
    for n in range(3):
        cols = slice(384 * n, 384 * n + 384)
        right = slabs[:, :, cols].reshape(HEADS * SLAB, 384)
        value = dot32(left, right, ((1,), (0,))) + stream[:, cols].astype(jnp.float32)
        value = value.astype(jnp.bfloat16)
        out[:, cols] = value
        pooled.append(dot32(member, value, ((1,), (0,))))
    pooled = jnp.concatenate(pooled, axis=1) / counts
    unit = pooled / jnp.sqrt(jnp.sum(pooled * pooled, axis=1, keepdims=True) + 1e-6)
    images[pl.ds(c, 1), pl.ds(pair, 1)] = unit[0:3][None, None]

    def third(i, _):
        to, _ = peer_row(i)
        send(images.at[c, pair], images.at[c, pair], img_s, img_r, to)
        return 0

    lax.fori_loop(1, 16, third, 0)

    await_bytes(texts.at[pl.ds(0, 31)], text_r)
    table_t[...] = jnp.zeros(table_t.shape, table_t.dtype)
    for b in range(32):
        table_t[4 * b : 4 * b + 3, :] = texts[b].astype(jnp.float32)
    raw_text = table_t[...]
    norm = jnp.sqrt(jnp.sum(raw_text * raw_text, axis=1, keepdims=True) + 1e-6)
    text_unit = raw_text / norm
    table_i[...] = jnp.zeros(table_i.shape, table_i.dtype)

    await_bytes(images.at[c, pl.ds(0, 15)], img_r)
    forward = send(images.at[c], images.at[c], imf_s, imf_r, sibling)
    forward.wait_recv()
    for b in range(32):
        table_i[4 * b : 4 * b + 3, :] = images[b // 16, b % 16]
    image_unit = table_i[...]

    scale, bias = scale_ref[0], bias_ref[0]
    logits = scale * lax.dot_general(
        image_unit, text_unit, (((1,), (1,)), ((), ())), precision=HIGHEST, preferred_element_type=jnp.float32
    ) + bias
    ri = lax.broadcasted_iota(jnp.int32, (128, 128), 0)
    ci = lax.broadcasted_iota(jnp.int32, (128, 128), 1)
    me_row, me_col = 4 * (c * 16 + pair), 4 * dp
    diagonal = ((ri - me_row) == (ci - me_col)) & (ri >= me_row) & (ri < me_row + 4)
    sign = jnp.where(diagonal, jnp.float32(-1.0), jnp.float32(1.0))
    coef = sign / (1.0 + jnp.exp(-sign * logits))
    coef = jnp.where((ri % 4 < 3) & (ci % 4 < 3), scale * coef, jnp.float32(0.0))
    image_part = lax.dot_general(
        coef, text_unit, (((1,), (0,)), ((), ())), precision=HIGHEST, preferred_element_type=jnp.float32
    )
    table_i[...] = image_part
    for b in range(32):
        part_i[b // 16, b % 16] = table_i[4 * b : 4 * b + 3, :]
    swap = send(part_i.at[1 - c], part_x, mix_s, mix_r, sibling)
    text_part = lax.dot_general(
        coef, image_unit, (((0,), (0,)), ((), ())), precision=HIGHEST, preferred_element_type=jnp.float32
    )
    table_t[...] = text_part
    for b in range(32):
        sent_t[b] = table_t[4 * b : 4 * b + 3, :].astype(sent_t.dtype)

    def fourth(i, _):
        to, other = peer_col(i)
        send(sent_t.at[other], got_t.at[i - 1], gt_s, gt_r, to)
        return 0

    lax.fori_loop(1, 32, fourth, 0)

    swap.wait_recv()
    for b in range(16):
        sent_i[b] = (part_i[pl.ds(c, 1), b][0] + part_x[b]).astype(sent_i.dtype)

    def fifth(i, _):
        to, other = peer_row(i)
        send(sent_i.at[other], got_i.at[i - 1], gi_s, gi_r, to)
        return 0

    lax.fori_loop(1, 16, fifth, 0)

    total = part_i[pl.ds(c, 1), pl.ds(pair, 1)][0, 0] + part_x[pl.ds(pair, 1)][0]
    await_bytes(got_i, gi_r)
    for b in range(15):
        total = total + got_i[b].astype(jnp.float32)
    image_grad[...] = total
    total = sent_t[pl.ds(dp, 1)][0].astype(jnp.float32)
    await_bytes(got_t, gt_r)
    for b in range(31):
        total = total + got_t[b].astype(jnp.float32)
    text_grad[...] = total

    await_bytes(arrived, one_s)
    await_bytes(texts.at[pl.ds(0, 31)], text_s)
    for copy in copies + forwards:
        copy.wait_send()
    await_bytes(images.at[0, pl.ds(0, 15)], img_s)
    forward.wait_send()
    swap.wait_send()
    await_bytes(got_i, gi_s)
    await_bytes(got_t, gt_s)


def per_device(stream, query_key_value, lengths, out_weight, text_embed, logit_scale, logit_bias):
    any_space, vmem, smem = (
        pl.BlockSpec(memory_space=pl.ANY),
        pl.BlockSpec(memory_space=pltpu.VMEM),
        pl.BlockSpec(memory_space=pltpu.SMEM),
    )
    f32, bf16 = jnp.float32, jnp.bfloat16
    dma = pltpu.SemaphoreType.DMA
    return pl.pallas_call(
        kernel,
        out_shape=(
            jax.ShapeDtypeStruct((ROWS, D), bf16),
            jax.ShapeDtypeStruct((3, D), f32),
            jax.ShapeDtypeStruct((3, D), f32),
        ),
        in_specs=[smem, smem, smem, vmem, vmem, any_space, any_space],
        out_specs=(vmem, vmem, vmem),
        scratch_shapes=[
            pltpu.VMEM((ROWS, 3 * D), bf16),
            pltpu.VMEM((ROWS, D), bf16),
            pltpu.VMEM((2, 48, 128), bf16),
            pltpu.VMEM((72, 128), f32),
            pltpu.VMEM((24, 128), bf16),
            pltpu.VMEM((32, 24, 128), bf16),
            pltpu.VMEM((HEADS, SLAB, D), bf16),
            pltpu.VMEM((ROWS, HEADS * SLAB), bf16),
            pltpu.VMEM((32, 3, D), bf16),
            pltpu.VMEM((2, 16, 3, D), f32),
            pltpu.VMEM((128, D), f32),
            pltpu.VMEM((128, D), f32),
            pltpu.VMEM((2, 16, 3, D), f32),
            pltpu.VMEM((16, 3, D), f32),
            pltpu.VMEM((16, 3, D), bf16),
            pltpu.VMEM((15, 3, D), bf16),
            pltpu.VMEM((32, 3, D), bf16),
            pltpu.VMEM((31, 3, D), bf16),
            dma((2,)), dma, dma, dma, dma, dma((10,)), dma((10,)), dma((8,)), dma((8,)),
            dma, dma, dma, dma, dma, dma, dma, dma, dma, dma, dma, dma,
        ],
        compiler_params=pltpu.CompilerParams(
            collective_id=0, has_side_effects=True, vmem_limit_bytes=56 << 20
        ),
    )(lengths, logit_scale, logit_bias, out_weight, text_embed, query_key_value, stream)


def solution(mesh):
    both = P(("dp", "mp"), None)
    return jax.shard_map(
        per_device,
        mesh=mesh,
        in_specs=(both, both, both, P("mp", "dp"), both, P(), P()),
        out_specs=(both, both, both),
        check_vma=False,
    )
```

```python
import functools
import math

import jax
import jax.numpy as jnp
from jax import lax
from jax.experimental import pallas as pl
from jax.experimental.pallas import tpu as pltpu
from jax.sharding import PartitionSpec as P

MESH = pl.DeviceIdType.MESH
HEADS = 16
HEAD = 72
SLAB = 80
ROWS = 256
D = 1152
BLK = 36
STEPS = ((1, 0, 0, 1), (-1, 0, 0, -1), (0, 1, 0, 2), (0, -1, 0, -2), (0, 0, 1, 3), (0, 0, -1, -3))
FAR = ((0, 2, 0, 0, 256), (0, -2, 0, 256, 256), (1, 0, 1, 512, 384), (-1, 0, -1, 896, 256))


def place():
    dp, mp = lax.axis_index("dp"), lax.axis_index("mp")
    return dp // 4, 2 * (dp % 4) + (mp // 2) % 2, mp // 4, mp % 2


def device(x, y, z, c):
    return (x * 4 + y // 2, z * 4 + (y % 2) * 2 + c)


def step_from(x, y, z, c, sx, sy, sz):
    return device((x + sx + 8) % 8, (y + sy + 8) % 8, (z + sz + 8) % 8, c)


def send(src, dst, send_sem, recv_sem, to):
    copy = pltpu.make_async_remote_copy(
        src_ref=src, dst_ref=dst, send_sem=send_sem, recv_sem=recv_sem, device_id=to, device_id_type=MESH
    )
    copy.start()
    return copy


def await_bytes(ref, sem):
    pltpu.make_async_copy(ref, ref, sem).wait()


def shift_lanes(value, amount):
    amount = amount % 128
    return value if amount == 0 else pltpu.roll(value, amount, 1)


def split(value):
    high = value.astype(jnp.bfloat16)
    low = (value - high.astype(jnp.float32)).astype(jnp.bfloat16)
    return high, low


def dot32(a, b, dims):
    return lax.dot_general(a, b, (dims, ((), ())), preferred_element_type=jnp.float32)


def kernel(
    lengths, scale_ref, bias_ref, weight, text, qkv_hbm, stream_hbm,
    out, image_grad, text_grad,
    qkv, stream, raw, rows72, packed, arrived, slabs, context, product,
    texts, images, table_i, table_t,
    part_i, part_x, sent_i, got_i, sent_t, got_t,
    local_sem, raw_s, raw_r, one_s, one_r, two_s, two_r, fwd_s, fwd_r,
    text_s, text_r, img_s, img_r, imf_s, imf_r, mix_s, mix_r, gi_s, gi_r, gt_s, gt_r,
):
    x, y, z, c = place()
    dp, mp = lax.axis_index("dp"), lax.axis_index("mp")
    yh, yl = y // 2, y % 2
    pair = z * 2 + yl
    sibling = device(x, y, z, 1 - c)
    mine = (x + 2 * y + 3 * z) % 8

    load_qkv = pltpu.make_async_copy(qkv_hbm, qkv, local_sem.at[0])
    load_qkv.start()
    load_stream = pltpu.make_async_copy(stream_hbm, stream, local_sem.at[1])
    load_stream.start()

    raw[...] = jnp.zeros(raw.shape, raw.dtype)
    raw[pl.ds(c, 1), 0:BLK, 0:BLK] = weight[...][None]

    with jax.named_scope("entry"):
        barrier = pltpu.get_barrier_semaphore()

        def greet(to):
            pl.semaphore_signal(barrier, inc=1, device_id=to, device_id_type=MESH)

        def source_of(i):
            return (i, mine * 4 + c * 2 + 1 - yl)

        def target_of(i):
            th, tz = lax.rem(yh + lax.div(i, 8), 4), lax.rem(z + i, 8)
            tx = lax.rem(z + 64 - 4 * th - 2 * (1 - c) - 3 * tz, 8)
            return (tx * 4 + th, tz * 4 + (1 - c) * 2 + yl)

        def peer_row(i):
            other = lax.rem(pair + i, 16)
            return (dp, 2 * other + c), other

        def peer_col(i):
            other = lax.rem(dp + i, 32)
            return (other, mp), other

        lax.fori_loop(0, 32, lambda i, _: (greet(source_of(i)), 0)[1], 0)
        greet(sibling)
        for sx, sy, sz, _ in STEPS:
            greet(step_from(x, y, z, c, sx, sy, sz))
        for sx, sy, sz, _, _ in FAR:
            greet(step_from(x, y, z, c, sx, sy, sz))
        lax.fori_loop(1, 16, lambda i, _: (greet(peer_row(i)[0]), 0)[1], 0)
        lax.fori_loop(1, 32, lambda i, _: (greet(peer_col(i)[0]), 0)[1], 0)
        pl.semaphore_wait(barrier, 1 + 32 + 6 + 4 + 15 + 31)

    with jax.named_scope("pack"):
        copy = send(raw.at[c], raw.at[c], raw_s, raw_r, sibling)
        copy.wait()
        rows72[0:BLK, :] = raw[0, 0:BLK, :].astype(jnp.float32)
        rows72[BLK : 2 * BLK, :] = raw[1, 0:BLK, :].astype(jnp.float32)
        lane = lax.broadcasted_iota(jnp.int32, (24, 128), 1)
        together = rows72[0:24, :]
        for g in (1, 2):
            piece = shift_lanes(rows72[24 * g : 24 * g + 24, :], BLK * g)
            together = jnp.where((lane >= BLK * g) & (lane < BLK * g + BLK), piece, together)
        packed[...] = together.astype(jnp.bfloat16)

    with jax.named_scope("first_start"):
        def first(i, _):
            send(packed, arrived.at[dp], one_s, one_r, target_of(i))
            return 0

        lax.fori_loop(0, 32, first, 0)

    with jax.named_scope("attention"):
        count0, count1, count2 = lengths[0, 0], lengths[0, 1], lengths[0, 2]

        def segment(shape, dim):
            at = lax.broadcasted_iota(jnp.int32, shape, dim)
            return (at >= count0).astype(jnp.int32) + (at >= count0 + count1).astype(jnp.int32)

        same = segment((ROWS, ROWS), 0) == segment((ROWS, ROWS), 1)
        load_qkv.wait()
        root = 1.0 / math.sqrt(HEAD)
        context[...] = jnp.zeros(context.shape, context.dtype)
        for h in range(HEADS):
            q = qkv[:, HEAD * h : HEAD * (h + 1)]
            k = qkv[:, D + HEAD * h : D + HEAD * (h + 1)]
            v = qkv[:, 2 * D + HEAD * h : 2 * D + HEAD * (h + 1)]
            scores = jnp.where(same, dot32(q, k, ((1,), (1,))) * root, jnp.float32(-1e30))
            raised = jnp.exp(scores - jnp.max(scores, axis=1, keepdims=True))
            total = jnp.sum(raised, axis=1, keepdims=True)
            attention = (raised / total).astype(jnp.bfloat16)
            mixed = dot32(attention, v, ((1,), (0,)))
            at = SLAB * (h // 2)
            context[h % 2, :, at : at + HEAD] = mixed.astype(jnp.bfloat16)

    with jax.named_scope("collect"):
        await_bytes(arrived, one_r)
        lane = lax.broadcasted_iota(jnp.int32, (24, 128), 1)
        bands = []
        for g in range(3):
            tiles = [None] * 9
            for d in range(32):
                piece = shift_lanes(arrived[d].astype(jnp.float32), BLK * d - BLK * g)
                for t in range(BLK * d // 128, (BLK * d + BLK - 1) // 128 + 1):
                    at = lane + 128 * t
                    keep = at >= BLK * d
                    tiles[t] = piece if tiles[t] is None else jnp.where(keep, piece, tiles[t])
            bands.append(jnp.concatenate(tiles, axis=1))
        bands.append(jnp.zeros((8, D), jnp.float32))
        slabs[pl.ds(c, 1), pl.ds(mine, 1)] = jnp.concatenate(bands, axis=0).astype(jnp.bfloat16)[None, None]
        own = slabs.at[c, mine]

    with jax.named_scope("swap_slabs"):
        copies = []
        for i, (sx, sy, sz, _) in enumerate(STEPS):
            to = step_from(x, y, z, c, sx, sy, sz)
            copies.append(send(own, own, two_s.at[i], two_r.at[i], to))
        for i, (sx, sy, sz, start, size) in enumerate(FAR):
            to = step_from(x, y, z, c, sx, sy, sz)
            part = slabs.at[c, mine, :, pl.ds(start, size)]
            copies.append(send(part, part, two_s.at[6 + i], two_r.at[6 + i], to))
        forwards = [send(own, own, fwd_s.at[0], fwd_r.at[0], sibling)]

        texts[pl.ds(dp, 1)] = text[...][None]

        def second(i, _):
            to, _ = peer_col(i)
            send(text, texts.at[dp], text_s, text_r, to)
            return 0

        lax.fori_loop(1, 32, second, 0)

        for i, (_, _, _, label) in enumerate(STEPS):
            copies[i].wait_recv()
            come = slabs.at[c, lax.rem(mine - label + 8, 8)]
            forwards.append(send(come, come, fwd_s.at[1 + i], fwd_r.at[1 + i], sibling))
        for i in range(6, 10):
            copies[i].wait_recv()
        come = slabs.at[c, lax.rem(mine + 4, 8)]
        forwards.append(send(come, come, fwd_s.at[7], fwd_r.at[7], sibling))

    with jax.named_scope("project"):
        load_stream.wait()
        numbers = lax.broadcasted_iota(jnp.int32, (8, ROWS), 0)
        member = (segment((8, ROWS), 1) == numbers).astype(jnp.bfloat16)
        row = lax.broadcasted_iota(jnp.int32, (8, 1), 0)
        counts = jnp.where(row == 0, count0, jnp.where(row == 1, count1, count2)).astype(jnp.float32)
        half = context[pl.ds(c, 1)][0]
        for n in range(3):
            cols = slice(384 * n, 384 * n + 384)
            right = slabs[pl.ds(c, 1), :, :, cols].reshape(HEADS // 2 * SLAB, 384)
            product[:, cols] = dot32(half, right, ((1,), (0,))) + stream[:, cols].astype(jnp.float32)
        for copy in forwards:
            copy.wait_recv()
        half = context[pl.ds(1 - c, 1)][0]
        pooled = []
        for n in range(3):
            cols = slice(384 * n, 384 * n + 384)
            right = slabs[pl.ds(1 - c, 1), :, :, cols].reshape(HEADS // 2 * SLAB, 384)
            value = (product[:, cols] + dot32(half, right, ((1,), (0,)))).astype(jnp.bfloat16)
            out[:, cols] = value
            pooled.append(dot32(member, value, ((1,), (0,))))
        pooled = jnp.concatenate(pooled, axis=1) / counts
        unit = pooled / jnp.sqrt(jnp.sum(pooled * pooled, axis=1, keepdims=True) + 1e-6)
        images[pl.ds(c, 1), pl.ds(pair, 1)] = unit[0:3].astype(jnp.bfloat16)[None, None]

    with jax.named_scope("images_start"):
        def third(i, _):
            to, _ = peer_row(i)
            send(images.at[c, pair], images.at[c, pair], img_s, img_r, to)
            return 0

        lax.fori_loop(1, 16, third, 0)

    with jax.named_scope("text_table"):
        await_bytes(texts.at[pl.ds(0, 31)], text_r)
        table_t[...] = jnp.zeros(table_t.shape, table_t.dtype)
        for b in range(32):
            table_t[4 * b : 4 * b + 3, :] = texts[b].astype(jnp.float32)
        raw_text = table_t[...]
        norm = jnp.sqrt(jnp.sum(raw_text * raw_text, axis=1, keepdims=True) + 1e-6)
        text_rows = raw_text.astype(jnp.bfloat16)
        scale, bias = scale_ref[0, 0], bias_ref[0, 0]

        own_image, own_text = unit[0:3], text[...].astype(jnp.float32)
        own_text = own_text / jnp.sqrt(jnp.sum(own_text * own_text, axis=1, keepdims=True) + 1e-6)
        match = scale * jnp.sum(own_image * own_text, axis=1, keepdims=True) + bias
        match = -scale / (1.0 + jnp.exp(match))
        image_grad[...] = match * own_text
        text_grad[...] = match * own_image
        table_i[...] = jnp.zeros(table_i.shape, table_i.dtype)

    with jax.named_scope("images_wait"):
        await_bytes(images.at[c, pl.ds(0, 15)], img_r)
        forward = send(images.at[c], images.at[c], imf_s, imf_r, sibling)
        forward.wait_recv()
        for b in range(32):
            table_i[4 * b : 4 * b + 3, :] = images[b // 16, b % 16].astype(jnp.float32)
        image_rows = table_i[...].astype(jnp.bfloat16)

    with jax.named_scope("coefficients"):
        logits = scale * (dot32(text_rows, image_rows, ((1,), (1,))) / norm) + bias
        ri = lax.broadcasted_iota(jnp.int32, (128, 128), 0)
        ci = lax.broadcasted_iota(jnp.int32, (128, 128), 1)
        me_row, me_col = 4 * dp, 4 * (c * 16 + pair)
        own = ((ri - me_row) == (ci - me_col)) & (ri >= me_row) & (ri < me_row + 4)
        coef = jnp.where(own | (ri % 4 == 3) | (ci % 4 == 3), jnp.float32(0.0), scale / (1.0 + jnp.exp(-logits)))

    with jax.named_scope("text_partials"):
        high, low = split(coef)
        table_t[...] = dot32(high, image_rows, ((1,), (0,))) + dot32(low, image_rows, ((1,), (0,)))
        for b in range(32):
            sent_t[b] = table_t[4 * b : 4 * b + 3, :].astype(sent_t.dtype)

        def fourth(i, _):
            to, other = peer_col(i)
            send(sent_t.at[other], got_t.at[i - 1], gt_s, gt_r, to)
            return 0

        lax.fori_loop(1, 32, fourth, 0)

    with jax.named_scope("image_partials"):
        high, low = split(coef / norm)
        table_i[...] = dot32(high, text_rows, ((0,), (0,))) + dot32(low, text_rows, ((0,), (0,)))
        for b in range(32):
            part_i[b // 16, b % 16] = table_i[4 * b : 4 * b + 3, :]
        swap = send(part_i.at[1 - c], part_x, mix_s, mix_r, sibling)

    with jax.named_scope("core_sum"):
        swap.wait_recv()
        for b in range(16):
            sent_i[b] = (part_i[pl.ds(c, 1), b][0] + part_x[b]).astype(sent_i.dtype)

        def fifth(i, _):
            to, other = peer_row(i)
            send(sent_i.at[other], got_i.at[i - 1], gi_s, gi_r, to)
            return 0

        lax.fori_loop(1, 16, fifth, 0)

    with jax.named_scope("image_total"):
        total = image_grad[...] + part_i[pl.ds(c, 1), pl.ds(pair, 1)][0, 0] + part_x[pl.ds(pair, 1)][0]
        await_bytes(got_i, gi_r)
        for b in range(15):
            total = total + got_i[b].astype(jnp.float32)
        image_grad[...] = total
    with jax.named_scope("text_total"):
        total = text_grad[...] + sent_t[pl.ds(dp, 1)][0].astype(jnp.float32)
        await_bytes(got_t, gt_r)
        for b in range(31):
            total = total + got_t[b].astype(jnp.float32)
        text_grad[...] = total

    with jax.named_scope("drain"):
        await_bytes(arrived, one_s)
        await_bytes(texts.at[pl.ds(0, 31)], text_s)
        for copy in copies + forwards:
            copy.wait_send()
        await_bytes(images.at[0, pl.ds(0, 15)], img_s)
        forward.wait_send()
        swap.wait_send()
        await_bytes(got_i, gi_s)
        await_bytes(got_t, gt_s)


def hand_out(mixed, image_part, text_part, out, image_grad, text_grad):
    out[...] = mixed[...]
    image_grad[...] = image_part[...]
    text_grad[...] = text_part[...]


def per_device(stream, query_key_value, lengths, out_weight, text_embed, logit_scale, logit_bias):
    any_space, vmem, smem = (
        pl.BlockSpec(memory_space=pl.ANY),
        pl.BlockSpec(memory_space=pltpu.VMEM),
        pl.BlockSpec(memory_space=pltpu.SMEM),
    )
    f32, bf16 = jnp.float32, jnp.bfloat16
    dma = pltpu.SemaphoreType.DMA
    results = pl.pallas_call(
        kernel,
        out_shape=(
            jax.ShapeDtypeStruct((ROWS, D), bf16),
            jax.ShapeDtypeStruct((3, D), f32),
            jax.ShapeDtypeStruct((3, D), f32),
        ),
        in_specs=[smem, smem, smem, vmem, vmem, any_space, any_space],
        out_specs=(vmem, vmem, vmem),
        scratch_shapes=[
            pltpu.VMEM((ROWS, 3 * D), bf16),
            pltpu.VMEM((ROWS, D), bf16),
            pltpu.VMEM((2, 48, 128), bf16),
            pltpu.VMEM((72, 128), f32),
            pltpu.VMEM((24, 128), bf16),
            pltpu.VMEM((32, 24, 128), bf16),
            pltpu.VMEM((2, HEADS // 2, SLAB, D), bf16),
            pltpu.VMEM((2, ROWS, HEADS // 2 * SLAB), bf16),
            pltpu.VMEM((ROWS, D), f32),
            pltpu.VMEM((32, 3, D), bf16),
            pltpu.VMEM((2, 16, 3, D), bf16),
            pltpu.VMEM((128, D), f32),
            pltpu.VMEM((128, D), f32),
            pltpu.VMEM((2, 16, 3, D), f32),
            pltpu.VMEM((16, 3, D), f32),
            pltpu.VMEM((16, 3, D), bf16),
            pltpu.VMEM((15, 3, D), bf16),
            pltpu.VMEM((32, 3, D), bf16),
            pltpu.VMEM((31, 3, D), bf16),
            dma((2,)), dma, dma, dma, dma, dma((10,)), dma((10,)), dma((8,)), dma((8,)),
            dma, dma, dma, dma, dma, dma, dma, dma, dma, dma, dma, dma,
        ],
        compiler_params=pltpu.CompilerParams(
            collective_id=0, has_side_effects=True, vmem_limit_bytes=56 << 20
        ),
    )(lengths, logit_scale.reshape(1, 1), logit_bias.reshape(1, 1), out_weight, text_embed, query_key_value, stream)
    return pl.pallas_call(
        hand_out,
        out_shape=tuple(jax.ShapeDtypeStruct(r.shape, r.dtype) for r in results),
        in_specs=[vmem] * 3,
        out_specs=(vmem,) * 3,
        compiler_params=pltpu.CompilerParams(vmem_limit_bytes=56 << 20),
    )(*results)


def solution(mesh):
    both = P(("dp", "mp"), None)
    return jax.shard_map(
        per_device,
        mesh=mesh,
        in_specs=(both, both, both, P("mp", "dp"), both, P(), P()),
        out_specs=(both, both, both),
        check_vma=False,
    )
```

```python
import functools
import math

import jax
import jax.numpy as jnp
from jax import lax
from jax.experimental import pallas as pl
from jax.experimental.pallas import tpu as pltpu
from jax.sharding import PartitionSpec as P

MESH = pl.DeviceIdType.MESH
HEADS = 16
HEAD = 72
SLAB = 80
ROWS = 256
D = 1152
BLK = 36
STEPS = ((1, 0, 0, 1), (-1, 0, 0, -1), (0, 1, 0, 2), (0, -1, 0, -2), (0, 0, 1, 3), (0, 0, -1, -3))
FAR = ((0, 2, 0, 0, 256), (0, -2, 0, 256, 256), (1, 0, 1, 512, 384), (-1, 0, -1, 896, 256))


def place():
    dp, mp = lax.axis_index("dp"), lax.axis_index("mp")
    return dp // 4, 2 * (dp % 4) + (mp // 2) % 2, mp // 4, mp % 2


def device(x, y, z, c):
    return (x * 4 + y // 2, z * 4 + (y % 2) * 2 + c)


def step_from(x, y, z, c, sx, sy, sz):
    return device((x + sx + 8) % 8, (y + sy + 8) % 8, (z + sz + 8) % 8, c)


def send(src, dst, send_sem, recv_sem, to):
    copy = pltpu.make_async_remote_copy(
        src_ref=src, dst_ref=dst, send_sem=send_sem, recv_sem=recv_sem, device_id=to, device_id_type=MESH
    )
    copy.start()
    return copy


def await_bytes(ref, sem):
    pltpu.make_async_copy(ref, ref, sem).wait()


def shift_lanes(value, amount):
    amount = amount % 128
    return value if amount == 0 else pltpu.roll(value, amount, 1)


def split(value):
    high = value.astype(jnp.bfloat16)
    low = (value - high.astype(jnp.float32)).astype(jnp.bfloat16)
    return high, low


def dot32(a, b, dims):
    return lax.dot_general(a, b, (dims, ((), ())), preferred_element_type=jnp.float32)


def kernel(
    lengths, scale_ref, bias_ref, weight, text, qkv_hbm, stream_hbm,
    out, image_grad, text_grad,
    qkv, stream, raw, rows72, packed, arrived, slabs, context, product,
    texts, images, table_i, table_t,
    part_i, part_x, sent_i, got_i, sent_t, got_t,
    local_sem, raw_s, raw_r, one_s, one_r, two_s, two_r, fwd_s, fwd_r,
    text_s, text_r, img_s, img_r, imf_s, imf_r, mix_s, mix_r, gi_s, gi_r, gt_s, gt_r,
):
    x, y, z, c = place()
    dp, mp = lax.axis_index("dp"), lax.axis_index("mp")
    yh, yl = y // 2, y % 2
    pair = z * 2 + yl
    sibling = device(x, y, z, 1 - c)
    mine = (x + 2 * y + 3 * z) % 8

    load_qkv = pltpu.make_async_copy(qkv_hbm, qkv, local_sem.at[0])
    load_qkv.start()
    load_stream = pltpu.make_async_copy(stream_hbm, stream, local_sem.at[1])
    load_stream.start()

    raw[...] = jnp.zeros(raw.shape, raw.dtype)
    raw[pl.ds(c, 1), 0:BLK, 0:BLK] = weight[...][None]

    with jax.named_scope("entry"):
        barrier = pltpu.get_barrier_semaphore()

        def greet(to):
            pl.semaphore_signal(barrier, inc=1, device_id=to, device_id_type=MESH)

        def source_of(i):
            return (i, mine * 4 + c * 2 + 1 - yl)

        def target_of(i):
            th, tz = lax.rem(yh + lax.div(i, 8), 4), lax.rem(z + i, 8)
            tx = lax.rem(z + 64 - 4 * th - 2 * (1 - c) - 3 * tz, 8)
            return (tx * 4 + th, tz * 4 + (1 - c) * 2 + yl)

        def peer_row(i):
            other = lax.rem(pair + i, 16)
            return (dp, 2 * other + c), other

        def peer_col(i):
            other = lax.rem(dp + i, 32)
            return (other, mp), other

        lax.fori_loop(0, 32, lambda i, _: (greet(source_of(i)), 0)[1], 0)
        greet(sibling)
        for sx, sy, sz, _ in STEPS:
            greet(step_from(x, y, z, c, sx, sy, sz))
        for sx, sy, sz, _, _ in FAR:
            greet(step_from(x, y, z, c, sx, sy, sz))
        lax.fori_loop(1, 16, lambda i, _: (greet(peer_row(i)[0]), 0)[1], 0)
        lax.fori_loop(1, 32, lambda i, _: (greet(peer_col(i)[0]), 0)[1], 0)
        pl.semaphore_wait(barrier, 1 + 32 + 6 + 4 + 15 + 31)

    with jax.named_scope("pack"):
        copy = send(raw.at[c], raw.at[c], raw_s, raw_r, sibling)
        copy.wait()
        rows72[0:BLK, :] = raw[0, 0:BLK, :].astype(jnp.float32)
        rows72[BLK : 2 * BLK, :] = raw[1, 0:BLK, :].astype(jnp.float32)
        lane = lax.broadcasted_iota(jnp.int32, (24, 128), 1)
        together = rows72[0:24, :]
        for g in (1, 2):
            piece = shift_lanes(rows72[24 * g : 24 * g + 24, :], BLK * g)
            together = jnp.where((lane >= BLK * g) & (lane < BLK * g + BLK), piece, together)
        packed[...] = together.astype(jnp.bfloat16)

    with jax.named_scope("first_start"):
        def first(i, _):
            send(packed, arrived.at[dp], one_s, one_r, target_of(i))
            return 0

        lax.fori_loop(0, 32, first, 0)

    with jax.named_scope("attention"):
        count0, count1, count2 = lengths[0, 0], lengths[0, 1], lengths[0, 2]

        def segment(shape, dim):
            at = lax.broadcasted_iota(jnp.int32, shape, dim)
            return (at >= count0).astype(jnp.int32) + (at >= count0 + count1).astype(jnp.int32)

        same = segment((ROWS, ROWS), 0) == segment((ROWS, ROWS), 1)
        load_qkv.wait()
        root = 1.0 / math.sqrt(HEAD)
        context[...] = jnp.zeros(context.shape, context.dtype)

        def attend(heads):
            for h in heads:
                q = qkv[:, HEAD * h : HEAD * (h + 1)]
                k = qkv[:, D + HEAD * h : D + HEAD * (h + 1)]
                v = qkv[:, 2 * D + HEAD * h : 2 * D + HEAD * (h + 1)]
                scores = jnp.where(same, dot32(q, k, ((1,), (1,))) * root, jnp.float32(-1e30))
                raised = jnp.exp(scores - jnp.max(scores, axis=1, keepdims=True))
                total = jnp.sum(raised, axis=1, keepdims=True)
                attention = (raised / total).astype(jnp.bfloat16)
                mixed = dot32(attention, v, ((1,), (0,)))
                at = SLAB * (h // 2)
                context[h % 2, :, at : at + HEAD] = mixed.astype(jnp.bfloat16)

        attend(range(HEADS // 2))

    with jax.named_scope("collect"):
        await_bytes(arrived, one_r)
        lane = lax.broadcasted_iota(jnp.int32, (24, 128), 1)
        bands = []
        for g in range(3):
            tiles = [None] * 9
            for d in range(32):
                piece = shift_lanes(arrived[d].astype(jnp.float32), BLK * d - BLK * g)
                for t in range(BLK * d // 128, (BLK * d + BLK - 1) // 128 + 1):
                    at = lane + 128 * t
                    keep = at >= BLK * d
                    tiles[t] = piece if tiles[t] is None else jnp.where(keep, piece, tiles[t])
            bands.append(jnp.concatenate(tiles, axis=1))
        bands.append(jnp.zeros((8, D), jnp.float32))
        slabs[pl.ds(c, 1), pl.ds(mine, 1)] = jnp.concatenate(bands, axis=0).astype(jnp.bfloat16)[None, None]
        own = slabs.at[c, mine]

    with jax.named_scope("swap_slabs"):
        copies = []
        for i, (sx, sy, sz, _) in enumerate(STEPS):
            to = step_from(x, y, z, c, sx, sy, sz)
            copies.append(send(own, own, two_s.at[i], two_r.at[i], to))
        for i, (sx, sy, sz, start, size) in enumerate(FAR):
            to = step_from(x, y, z, c, sx, sy, sz)
            part = slabs.at[c, mine, :, pl.ds(start, size)]
            copies.append(send(part, part, two_s.at[6 + i], two_r.at[6 + i], to))
        forwards = [send(own, own, fwd_s.at[0], fwd_r.at[0], sibling)]

        texts[pl.ds(dp, 1)] = text[...][None]

        def second(i, _):
            to, _ = peer_col(i)
            send(text, texts.at[dp], text_s, text_r, to)
            return 0

        lax.fori_loop(1, 32, second, 0)

        attend(range(HEADS // 2, HEADS))
        for i, (_, _, _, label) in enumerate(STEPS):
            copies[i].wait_recv()
            come = slabs.at[c, lax.rem(mine - label + 8, 8)]
            forwards.append(send(come, come, fwd_s.at[1 + i], fwd_r.at[1 + i], sibling))
        for i in range(6, 10):
            copies[i].wait_recv()
        come = slabs.at[c, lax.rem(mine + 4, 8)]
        forwards.append(send(come, come, fwd_s.at[7], fwd_r.at[7], sibling))

    with jax.named_scope("project"):
        load_stream.wait()
        numbers = lax.broadcasted_iota(jnp.int32, (8, ROWS), 0)
        member = (segment((8, ROWS), 1) == numbers).astype(jnp.bfloat16)
        row = lax.broadcasted_iota(jnp.int32, (8, 1), 0)
        counts = jnp.where(row == 0, count0, jnp.where(row == 1, count1, count2)).astype(jnp.float32)
        half, rest = context[pl.ds(c, 1)][0], context[pl.ds(1 - c, 1)][0]
        pooled = dot32(member, stream[...], ((1,), (0,)))

        def pool(part, at):
            sums = dot32(member, part, ((1,), (0,)))
            high = sums.astype(jnp.bfloat16).astype(jnp.float32)
            both = jnp.concatenate([high, sums - high], axis=0).astype(jnp.bfloat16)
            pieces = [dot32(both, block(at, n), ((1,), (0,))) for n in range(3)]
            both = jnp.concatenate(pieces, axis=1)
            return both[0:8] + both[8:16]

        def block(at, n):
            return slabs[pl.ds(at, 1), :, :, 384 * n : 384 * n + 384].reshape(HEADS // 2 * SLAB, 384)

        pooled = pooled + pool(half, c)
        for n in range(3):
            cols = slice(384 * n, 384 * n + 384)
            product[:, cols] = dot32(half, block(c, n), ((1,), (0,))) + stream[:, cols].astype(jnp.float32)
        for copy in forwards:
            copy.wait_recv()
        pooled = (pooled + pool(rest, 1 - c)) / counts
        unit = pooled / jnp.sqrt(jnp.sum(pooled * pooled, axis=1, keepdims=True) + 1e-6)
        images[pl.ds(c, 1), pl.ds(pair, 1)] = unit[0:3].astype(jnp.bfloat16)[None, None]

    with jax.named_scope("images_start"):
        def third(i, _):
            to, _ = peer_row(i)
            send(images.at[c, pair], images.at[c, pair], img_s, img_r, to)
            return 0

        lax.fori_loop(1, 16, third, 0)

    with jax.named_scope("stream_out"):
        for n in range(3):
            cols = slice(384 * n, 384 * n + 384)
            out[:, cols] = (product[:, cols] + dot32(rest, block(1 - c, n), ((1,), (0,)))).astype(jnp.bfloat16)

    with jax.named_scope("text_table"):
        await_bytes(texts.at[pl.ds(0, 31)], text_r)
        table_t[...] = jnp.zeros(table_t.shape, table_t.dtype)
        for b in range(32):
            table_t[4 * b : 4 * b + 3, :] = texts[b].astype(jnp.float32)
        raw_text = table_t[...]
        norm = jnp.sqrt(jnp.sum(raw_text * raw_text, axis=1, keepdims=True) + 1e-6)
        text_rows = raw_text.astype(jnp.bfloat16)
        scale, bias = scale_ref[0, 0], bias_ref[0, 0]

        own_image, own_text = unit[0:3], text[...].astype(jnp.float32)
        own_text = own_text / jnp.sqrt(jnp.sum(own_text * own_text, axis=1, keepdims=True) + 1e-6)
        match = scale * jnp.sum(own_image * own_text, axis=1, keepdims=True) + bias
        match = -scale / (1.0 + jnp.exp(match))
        image_grad[...] = match * own_text
        text_grad[...] = match * own_image
        table_i[...] = jnp.zeros(table_i.shape, table_i.dtype)

    with jax.named_scope("images_wait"):
        await_bytes(images.at[c, pl.ds(0, 15)], img_r)
        forward = send(images.at[c], images.at[c], imf_s, imf_r, sibling)
        for b in range(16):
            table_i[pl.ds(c, 1), 4 * b : 4 * b + 3, :] = images[pl.ds(c, 1), b].astype(jnp.float32)
        forward.wait_recv()
        for b in range(16):
            table_i[pl.ds(1 - c, 1), 4 * b : 4 * b + 3, :] = images[pl.ds(1 - c, 1), b].astype(jnp.float32)
        image_rows = table_i[...].reshape(128, D).astype(jnp.bfloat16)

    with jax.named_scope("coefficients"):
        logits = scale * (dot32(text_rows, image_rows, ((1,), (1,))) / norm) + bias
        ri = lax.broadcasted_iota(jnp.int32, (128, 128), 0)
        ci = lax.broadcasted_iota(jnp.int32, (128, 128), 1)
        me_row, me_col = 4 * dp, 4 * (c * 16 + pair)
        own = ((ri - me_row) == (ci - me_col)) & (ri >= me_row) & (ri < me_row + 4)
        coef = jnp.where(own | (ri % 4 == 3) | (ci % 4 == 3), jnp.float32(0.0), scale / (1.0 + jnp.exp(-logits)))

    with jax.named_scope("text_partials"):
        high, low = split(coef)
        table_t[...] = dot32(high, image_rows, ((1,), (0,))) + dot32(low, image_rows, ((1,), (0,)))
        for b in range(32):
            sent_t[b] = table_t[4 * b : 4 * b + 3, :].astype(sent_t.dtype)

        def fourth(i, _):
            to, other = peer_col(i)
            send(sent_t.at[other], got_t.at[i - 1], gt_s, gt_r, to)
            return 0

        lax.fori_loop(1, 32, fourth, 0)

    with jax.named_scope("image_partials"):
        high, low = split(coef / norm)
        part = dot32(high, text_rows, ((0,), (0,))) + dot32(low, text_rows, ((0,), (0,)))
        table_i[...] = part.reshape(2, 64, D)
        for b in range(32):
            k = b % 16
            part_i[b // 16, k] = table_i[b // 16, 4 * k : 4 * k + 3, :]
        swap = send(part_i.at[1 - c], part_x, mix_s, mix_r, sibling)

    with jax.named_scope("core_sum"):
        swap.wait_recv()
        for b in range(16):
            sent_i[b] = (part_i[pl.ds(c, 1), b][0] + part_x[b]).astype(sent_i.dtype)

        def fifth(i, _):
            to, other = peer_row(i)
            send(sent_i.at[other], got_i.at[i - 1], gi_s, gi_r, to)
            return 0

        lax.fori_loop(1, 16, fifth, 0)

    with jax.named_scope("image_total"):
        total = image_grad[...] + part_i[pl.ds(c, 1), pl.ds(pair, 1)][0, 0] + part_x[pl.ds(pair, 1)][0]
        await_bytes(got_i, gi_r)
        for b in range(15):
            total = total + got_i[b].astype(jnp.float32)
        image_grad[...] = total
    with jax.named_scope("text_total"):
        total = text_grad[...] + sent_t[pl.ds(dp, 1)][0].astype(jnp.float32)
        await_bytes(got_t, gt_r)
        for b in range(31):
            total = total + got_t[b].astype(jnp.float32)
        text_grad[...] = total

    with jax.named_scope("drain"):
        await_bytes(arrived, one_s)
        await_bytes(texts.at[pl.ds(0, 31)], text_s)
        for copy in copies + forwards:
            copy.wait_send()
        await_bytes(images.at[0, pl.ds(0, 15)], img_s)
        forward.wait_send()
        swap.wait_send()
        await_bytes(got_i, gi_s)
        await_bytes(got_t, gt_s)


def hand_out(mixed, image_part, text_part, out, image_grad, text_grad):
    out[...] = mixed[...]
    image_grad[...] = image_part[...]
    text_grad[...] = text_part[...]


def per_device(stream, query_key_value, lengths, out_weight, text_embed, logit_scale, logit_bias):
    any_space, vmem, smem = (
        pl.BlockSpec(memory_space=pl.ANY),
        pl.BlockSpec(memory_space=pltpu.VMEM),
        pl.BlockSpec(memory_space=pltpu.SMEM),
    )
    f32, bf16 = jnp.float32, jnp.bfloat16
    dma = pltpu.SemaphoreType.DMA
    results = pl.pallas_call(
        kernel,
        out_shape=(
            jax.ShapeDtypeStruct((ROWS, D), bf16),
            jax.ShapeDtypeStruct((3, D), f32),
            jax.ShapeDtypeStruct((3, D), f32),
        ),
        in_specs=[smem, smem, smem, vmem, vmem, any_space, any_space],
        out_specs=(vmem, vmem, vmem),
        scratch_shapes=[
            pltpu.VMEM((ROWS, 3 * D), bf16),
            pltpu.VMEM((ROWS, D), bf16),
            pltpu.VMEM((2, 48, 128), bf16),
            pltpu.VMEM((72, 128), f32),
            pltpu.VMEM((24, 128), bf16),
            pltpu.VMEM((32, 24, 128), bf16),
            pltpu.VMEM((2, HEADS // 2, SLAB, D), bf16),
            pltpu.VMEM((2, ROWS, HEADS // 2 * SLAB), bf16),
            pltpu.VMEM((ROWS, D), f32),
            pltpu.VMEM((32, 3, D), bf16),
            pltpu.VMEM((2, 16, 3, D), bf16),
            pltpu.VMEM((2, 64, D), f32),
            pltpu.VMEM((128, D), f32),
            pltpu.VMEM((2, 16, 3, D), f32),
            pltpu.VMEM((16, 3, D), f32),
            pltpu.VMEM((16, 3, D), bf16),
            pltpu.VMEM((15, 3, D), bf16),
            pltpu.VMEM((32, 3, D), bf16),
            pltpu.VMEM((31, 3, D), bf16),
            dma((2,)), dma, dma, dma, dma, dma((10,)), dma((10,)), dma((8,)), dma((8,)),
            dma, dma, dma, dma, dma, dma, dma, dma, dma, dma, dma, dma,
        ],
        compiler_params=pltpu.CompilerParams(
            collective_id=0, has_side_effects=True, vmem_limit_bytes=56 << 20
        ),
    )(lengths, logit_scale.reshape(1, 1), logit_bias.reshape(1, 1), out_weight, text_embed, query_key_value, stream)
    return pl.pallas_call(
        hand_out,
        out_shape=tuple(jax.ShapeDtypeStruct(r.shape, r.dtype) for r in results),
        in_specs=[vmem] * 3,
        out_specs=(vmem,) * 3,
        compiler_params=pltpu.CompilerParams(vmem_limit_bytes=56 << 20),
    )(*results)


def solution(mesh):
    both = P(("dp", "mp"), None)
    return jax.shard_map(
        per_device,
        mesh=mesh,
        in_specs=(both, both, both, P("mp", "dp"), both, P(), P()),
        out_specs=(both, both, both),
        check_vma=False,
    )
```

```python
import functools
import math

import jax
import jax.numpy as jnp
from jax import lax
from jax.experimental import pallas as pl
from jax.experimental.pallas import tpu as pltpu
from jax.sharding import PartitionSpec as P

MESH = pl.DeviceIdType.MESH
HEADS = 16
HEAD = 72
SLAB = 80
ROWS = 256
D = 1152
BLK = 36
STEPS = ((1, 0, 0, 1), (-1, 0, 0, -1), (0, 1, 0, 2), (0, -1, 0, -2), (0, 0, 1, 3), (0, 0, -1, -3))
FAR = ((0, 2, 0, 0, 256), (0, -2, 0, 256, 256), (1, 0, 1, 512, 384), (-1, 0, -1, 896, 256))


def place():
    dp, mp = lax.axis_index("dp"), lax.axis_index("mp")
    return dp // 4, 2 * (dp % 4) + (mp // 2) % 2, mp // 4, mp % 2


def device(x, y, z, c):
    return (x * 4 + y // 2, z * 4 + (y % 2) * 2 + c)


def step_from(x, y, z, c, sx, sy, sz):
    return device((x + sx + 8) % 8, (y + sy + 8) % 8, (z + sz + 8) % 8, c)


def send(src, dst, send_sem, recv_sem, to):
    copy = pltpu.make_async_remote_copy(
        src_ref=src, dst_ref=dst, send_sem=send_sem, recv_sem=recv_sem, device_id=to, device_id_type=MESH
    )
    copy.start()
    return copy


def await_bytes(ref, sem):
    pltpu.make_async_copy(ref, ref, sem).wait()


def shift_lanes(value, amount):
    amount = amount % 128
    return value if amount == 0 else pltpu.roll(value, amount, 1)


def split(value):
    high = value.astype(jnp.bfloat16)
    low = (value - high.astype(jnp.float32)).astype(jnp.bfloat16)
    return high, low


def dot32(a, b, dims):
    return lax.dot_general(a, b, (dims, ((), ())), preferred_element_type=jnp.float32)


def kernel(
    lengths, scale_ref, bias_ref, weight, text, qkv_hbm, stream_hbm,
    out, image_grad, text_grad,
    qkv, stream, raw, rows72, packed, arrived, slabs, context, product,
    texts, images, table_i, table_t,
    part_i, part_x, sent_i, got_i, sent_t, got_t,
    local_sem, raw_s, raw_r, one_s, one_r, two_s, two_r, fwd_s, fwd_r,
    text_s, text_r, img_s, img_r, imf_s, imf_r, mix_s, mix_r, gi_s, gi_r, gt_s, gt_r,
):
    x, y, z, c = place()
    dp, mp = lax.axis_index("dp"), lax.axis_index("mp")
    yh, yl = y // 2, y % 2
    pair = z * 2 + yl
    sibling = device(x, y, z, 1 - c)
    mine = (x + 2 * y + 3 * z) % 8

    load_qkv = pltpu.make_async_copy(qkv_hbm, qkv, local_sem.at[0])
    load_qkv.start()
    load_stream = pltpu.make_async_copy(stream_hbm, stream, local_sem.at[1])
    load_stream.start()

    raw[...] = jnp.zeros(raw.shape, raw.dtype)
    raw[pl.ds(c, 1), 0:BLK, 0:BLK] = weight[...][None]

    with jax.named_scope("entry"):
        barrier = pltpu.get_barrier_semaphore()

        def greet(to):
            pl.semaphore_signal(barrier, inc=1, device_id=to, device_id_type=MESH)

        def source_of(i):
            return (lax.rem(dp + 14 + i, 32), mine * 4 + c * 2 + 1 - yl)

        def target_of(i):
            th, tz = lax.rem(yh + 2 + lax.div(i, 8), 4), lax.rem(z + 4 + i, 8)
            tx = lax.rem(z + 64 - 4 * th - 2 * (1 - c) - 3 * tz, 8)
            return (tx * 4 + th, tz * 4 + (1 - c) * 2 + yl)

        def peer_row(i):
            off = 1 + lax.rem(i + 6, 15)
            other = lax.rem(pair + off, 16)
            return (dp, 2 * other + c), other, off - 1

        def peer_col(i):
            off = 1 + lax.rem(i + 12, 31)
            other = lax.rem(dp + off, 32)
            return (other, mp), other, off - 1

        lax.fori_loop(0, 32, lambda i, _: (greet(source_of(i)), 0)[1], 0)
        greet(sibling)
        for sx, sy, sz, _ in STEPS:
            greet(step_from(x, y, z, c, sx, sy, sz))
        for sx, sy, sz, _, _ in FAR:
            greet(step_from(x, y, z, c, sx, sy, sz))
        lax.fori_loop(1, 16, lambda i, _: (greet(peer_row(i)[0]), 0)[1], 0)
        lax.fori_loop(1, 32, lambda i, _: (greet(peer_col(i)[0]), 0)[1], 0)
        pl.semaphore_wait(barrier, 1 + 32 + 6 + 4 + 15 + 31)

    with jax.named_scope("pack"):
        copy = send(raw.at[c], raw.at[c], raw_s, raw_r, sibling)
        copy.wait()
        rows72[0:BLK, :] = raw[0, 0:BLK, :].astype(jnp.float32)
        rows72[BLK : 2 * BLK, :] = raw[1, 0:BLK, :].astype(jnp.float32)
        lane = lax.broadcasted_iota(jnp.int32, (24, 128), 1)
        together = rows72[0:24, :]
        for g in (1, 2):
            piece = shift_lanes(rows72[24 * g : 24 * g + 24, :], BLK * g)
            together = jnp.where((lane >= BLK * g) & (lane < BLK * g + BLK), piece, together)
        packed[...] = together.astype(jnp.bfloat16)

    with jax.named_scope("first_start"):
        def first(i, _):
            send(packed, arrived.at[dp], one_s, one_r, target_of(i))
            return 0

        lax.fori_loop(0, 32, first, 0)

    with jax.named_scope("attention"):
        count0, count1, count2 = lengths[0, 0], lengths[0, 1], lengths[0, 2]

        def segment(shape, dim):
            at = lax.broadcasted_iota(jnp.int32, shape, dim)
            return (at >= count0).astype(jnp.int32) + (at >= count0 + count1).astype(jnp.int32)

        same = segment((ROWS, ROWS), 0) == segment((ROWS, ROWS), 1)
        load_qkv.wait()
        root = 1.0 / math.sqrt(HEAD)
        context[...] = jnp.zeros(context.shape, context.dtype)

        def attend(heads):
            for h in heads:
                q = qkv[:, HEAD * h : HEAD * (h + 1)]
                k = qkv[:, D + HEAD * h : D + HEAD * (h + 1)]
                v = qkv[:, 2 * D + HEAD * h : 2 * D + HEAD * (h + 1)]
                scores = jnp.where(same, dot32(q, k, ((1,), (1,))) * root, jnp.float32(-1e30))
                raised = jnp.exp(scores - jnp.max(scores, axis=1, keepdims=True))
                total = jnp.sum(raised, axis=1, keepdims=True)
                attention = (raised / total).astype(jnp.bfloat16)
                mixed = dot32(attention, v, ((1,), (0,)))
                at = SLAB * (h // 2)
                context[h % 2, :, at : at + HEAD] = mixed.astype(jnp.bfloat16)

        attend(range(HEADS // 2))

    with jax.named_scope("collect"):
        await_bytes(arrived, one_r)
        lane = lax.broadcasted_iota(jnp.int32, (24, 128), 1)
        bands = []
        for g in range(3):
            tiles = [None] * 9
            for d in range(32):
                piece = shift_lanes(arrived[d].astype(jnp.float32), BLK * d - BLK * g)
                for t in range(BLK * d // 128, (BLK * d + BLK - 1) // 128 + 1):
                    at = lane + 128 * t
                    keep = at >= BLK * d
                    tiles[t] = piece if tiles[t] is None else jnp.where(keep, piece, tiles[t])
            bands.append(jnp.concatenate(tiles, axis=1))
        bands.append(jnp.zeros((8, D), jnp.float32))
        slabs[pl.ds(c, 1), pl.ds(mine, 1)] = jnp.concatenate(bands, axis=0).astype(jnp.bfloat16)[None, None]
        own = slabs.at[c, mine]

    with jax.named_scope("swap_slabs"):
        copies, pieces = [], []
        for i, (sx, sy, sz, start, size) in enumerate(FAR):
            to = step_from(x, y, z, c, sx, sy, sz)
            part = slabs.at[c, mine, :, pl.ds(start, size)]
            pieces.append(send(part, part, two_s.at[6 + i], two_r.at[6 + i], to))
        for i, (sx, sy, sz, _) in enumerate(STEPS):
            to = step_from(x, y, z, c, sx, sy, sz)
            copies.append(send(own, own, two_s.at[i], two_r.at[i], to))
        forwards = [send(own, own, fwd_s.at[0], fwd_r.at[0], sibling)]

        texts[pl.ds(dp, 1)] = text[...][None]

        def second(i, _):
            to, _, _ = peer_col(i)
            send(text, texts.at[dp], text_s, text_r, to)
            return 0

        lax.fori_loop(1, 32, second, 0)

        attend(range(HEADS // 2, HEADS))
        for i, (_, _, _, label) in enumerate(STEPS):
            copies[i].wait_recv()
            come = slabs.at[c, lax.rem(mine - label + 8, 8)]
            forwards.append(send(come, come, fwd_s.at[1 + i], fwd_r.at[1 + i], sibling))
        for copy in pieces:
            copy.wait_recv()
        come = slabs.at[c, lax.rem(mine + 4, 8)]
        forwards.append(send(come, come, fwd_s.at[7], fwd_r.at[7], sibling))

    with jax.named_scope("project"):
        load_stream.wait()
        numbers = lax.broadcasted_iota(jnp.int32, (8, ROWS), 0)
        member = (segment((8, ROWS), 1) == numbers).astype(jnp.bfloat16)
        row = lax.broadcasted_iota(jnp.int32, (8, 1), 0)
        counts = jnp.where(row == 0, count0, jnp.where(row == 1, count1, count2)).astype(jnp.float32)
        half, rest = context[pl.ds(c, 1)][0], context[pl.ds(1 - c, 1)][0]
        pooled = dot32(member, stream[...], ((1,), (0,)))

        def pool(part, at):
            sums = dot32(member, part, ((1,), (0,)))
            high = sums.astype(jnp.bfloat16).astype(jnp.float32)
            both = jnp.concatenate([high, sums - high], axis=0).astype(jnp.bfloat16)
            pieces = [dot32(both, block(at, n), ((1,), (0,))) for n in range(3)]
            both = jnp.concatenate(pieces, axis=1)
            return both[0:8] + both[8:16]

        def block(at, n):
            return slabs[pl.ds(at, 1), :, :, 384 * n : 384 * n + 384].reshape(HEADS // 2 * SLAB, 384)

        pooled = pooled + pool(half, c)
        for n in range(3):
            cols = slice(384 * n, 384 * n + 384)
            product[:, cols] = dot32(half, block(c, n), ((1,), (0,))) + stream[:, cols].astype(jnp.float32)
        for copy in forwards:
            copy.wait_recv()
        pooled = (pooled + pool(rest, 1 - c)) / counts
        unit = pooled / jnp.sqrt(jnp.sum(pooled * pooled, axis=1, keepdims=True) + 1e-6)
        images[pl.ds(c, 1), pl.ds(pair, 1)] = unit[0:3].astype(jnp.bfloat16)[None, None]

    with jax.named_scope("images_start"):
        def third(i, _):
            to, _, _ = peer_row(i)
            send(images.at[c, pair], images.at[c, pair], img_s, img_r, to)
            return 0

        lax.fori_loop(1, 16, third, 0)

    with jax.named_scope("stream_out"):
        for n in range(3):
            cols = slice(384 * n, 384 * n + 384)
            out[:, cols] = (product[:, cols] + dot32(rest, block(1 - c, n), ((1,), (0,)))).astype(jnp.bfloat16)

    with jax.named_scope("text_table"):
        await_bytes(texts.at[pl.ds(0, 31)], text_r)
        table_t[...] = jnp.zeros(table_t.shape, table_t.dtype)
        for b in range(32):
            table_t[4 * b : 4 * b + 3, :] = texts[b].astype(jnp.float32)
        raw_text = table_t[...]
        norm = jnp.sqrt(jnp.sum(raw_text * raw_text, axis=1, keepdims=True) + 1e-6)
        text_rows = raw_text.astype(jnp.bfloat16)
        scale, bias = scale_ref[0, 0], bias_ref[0, 0]

        own_image, own_text = unit[0:3], text[...].astype(jnp.float32)
        own_text = own_text / jnp.sqrt(jnp.sum(own_text * own_text, axis=1, keepdims=True) + 1e-6)
        match = scale * jnp.sum(own_image * own_text, axis=1, keepdims=True) + bias
        match = -scale / (1.0 + jnp.exp(match))
        image_grad[...] = match * own_text
        text_grad[...] = match * own_image
        table_i[...] = jnp.zeros(table_i.shape, table_i.dtype)

    with jax.named_scope("images_wait"):
        await_bytes(images.at[c, pl.ds(0, 15)], img_r)
        forward = send(images.at[c], images.at[c], imf_s, imf_r, sibling)
        for b in range(16):
            table_i[pl.ds(c, 1), 4 * b : 4 * b + 3, :] = images[pl.ds(c, 1), b].astype(jnp.float32)
        forward.wait_recv()
        for b in range(16):
            table_i[pl.ds(1 - c, 1), 4 * b : 4 * b + 3, :] = images[pl.ds(1 - c, 1), b].astype(jnp.float32)
        image_rows = table_i[...].reshape(128, D).astype(jnp.bfloat16)

    with jax.named_scope("coefficients"):
        logits = scale * (dot32(text_rows, image_rows, ((1,), (1,))) / norm) + bias
        ri = lax.broadcasted_iota(jnp.int32, (128, 128), 0)
        ci = lax.broadcasted_iota(jnp.int32, (128, 128), 1)
        me_row, me_col = 4 * dp, 4 * (c * 16 + pair)
        own = ((ri - me_row) == (ci - me_col)) & (ri >= me_row) & (ri < me_row + 4)
        coef = jnp.where(own | (ri % 4 == 3) | (ci % 4 == 3), jnp.float32(0.0), scale / (1.0 + jnp.exp(-logits)))

    with jax.named_scope("text_partials"):
        high, low = split(coef)
        table_t[...] = dot32(high, image_rows, ((1,), (0,))) + dot32(low, image_rows, ((1,), (0,)))
        for b in range(32):
            sent_t[b] = table_t[4 * b : 4 * b + 3, :].astype(sent_t.dtype)

        def fourth(i, _):
            to, other, slot = peer_col(i)
            send(sent_t.at[other], got_t.at[slot], gt_s, gt_r, to)
            return 0

        lax.fori_loop(1, 32, fourth, 0)

    with jax.named_scope("image_partials"):
        high, low = split(coef / norm)
        part = dot32(high, text_rows, ((0,), (0,))) + dot32(low, text_rows, ((0,), (0,)))
        table_i[...] = part.reshape(2, 64, D)
        for b in range(32):
            k = b % 16
            part_i[b // 16, k] = table_i[b // 16, 4 * k : 4 * k + 3, :]
        swap = send(part_i.at[1 - c], part_x, mix_s, mix_r, sibling)

    with jax.named_scope("core_sum"):
        swap.wait_recv()
        for b in range(16):
            sent_i[b] = (part_i[pl.ds(c, 1), b][0] + part_x[b]).astype(sent_i.dtype)

        def fifth(i, _):
            to, other, slot = peer_row(i)
            send(sent_i.at[other], got_i.at[slot], gi_s, gi_r, to)
            return 0

        lax.fori_loop(1, 16, fifth, 0)

    with jax.named_scope("image_total"):
        total = image_grad[...] + part_i[pl.ds(c, 1), pl.ds(pair, 1)][0, 0] + part_x[pl.ds(pair, 1)][0]
        await_bytes(got_i, gi_r)
        for b in range(15):
            total = total + got_i[b].astype(jnp.float32)
        image_grad[...] = total
    with jax.named_scope("text_total"):
        total = text_grad[...] + sent_t[pl.ds(dp, 1)][0].astype(jnp.float32)
        await_bytes(got_t, gt_r)
        for b in range(31):
            total = total + got_t[b].astype(jnp.float32)
        text_grad[...] = total

    with jax.named_scope("drain"):
        await_bytes(arrived, one_s)
        await_bytes(texts.at[pl.ds(0, 31)], text_s)
        for copy in copies + pieces + forwards:
            copy.wait_send()
        await_bytes(images.at[0, pl.ds(0, 15)], img_s)
        forward.wait_send()
        swap.wait_send()
        await_bytes(got_i, gi_s)
        await_bytes(got_t, gt_s)


def hand_out(mixed, image_part, text_part, out, image_grad, text_grad):
    out[...] = mixed[...]
    image_grad[...] = image_part[...]
    text_grad[...] = text_part[...]


def per_device(stream, query_key_value, lengths, out_weight, text_embed, logit_scale, logit_bias):
    any_space, vmem, smem = (
        pl.BlockSpec(memory_space=pl.ANY),
        pl.BlockSpec(memory_space=pltpu.VMEM),
        pl.BlockSpec(memory_space=pltpu.SMEM),
    )
    f32, bf16 = jnp.float32, jnp.bfloat16
    dma = pltpu.SemaphoreType.DMA
    results = pl.pallas_call(
        kernel,
        out_shape=(
            jax.ShapeDtypeStruct((ROWS, D), bf16),
            jax.ShapeDtypeStruct((3, D), f32),
            jax.ShapeDtypeStruct((3, D), f32),
        ),
        in_specs=[smem, smem, smem, vmem, vmem, any_space, any_space],
        out_specs=(vmem, vmem, vmem),
        scratch_shapes=[
            pltpu.VMEM((ROWS, 3 * D), bf16),
            pltpu.VMEM((ROWS, D), bf16),
            pltpu.VMEM((2, 48, 128), bf16),
            pltpu.VMEM((72, 128), f32),
            pltpu.VMEM((24, 128), bf16),
            pltpu.VMEM((32, 24, 128), bf16),
            pltpu.VMEM((2, HEADS // 2, SLAB, D), bf16),
            pltpu.VMEM((2, ROWS, HEADS // 2 * SLAB), bf16),
            pltpu.VMEM((ROWS, D), f32),
            pltpu.VMEM((32, 3, D), bf16),
            pltpu.VMEM((2, 16, 3, D), bf16),
            pltpu.VMEM((2, 64, D), f32),
            pltpu.VMEM((128, D), f32),
            pltpu.VMEM((2, 16, 3, D), f32),
            pltpu.VMEM((16, 3, D), f32),
            pltpu.VMEM((16, 3, D), bf16),
            pltpu.VMEM((15, 3, D), bf16),
            pltpu.VMEM((32, 3, D), bf16),
            pltpu.VMEM((31, 3, D), bf16),
            dma((2,)), dma, dma, dma, dma, dma((10,)), dma((10,)), dma((8,)), dma((8,)),
            dma, dma, dma, dma, dma, dma, dma, dma, dma, dma, dma, dma,
        ],
        compiler_params=pltpu.CompilerParams(
            collective_id=0, has_side_effects=True, vmem_limit_bytes=56 << 20
        ),
    )(lengths, logit_scale.reshape(1, 1), logit_bias.reshape(1, 1), out_weight, text_embed, query_key_value, stream)
    return pl.pallas_call(
        hand_out,
        out_shape=tuple(jax.ShapeDtypeStruct(r.shape, r.dtype) for r in results),
        in_specs=[vmem] * 3,
        out_specs=(vmem,) * 3,
        compiler_params=pltpu.CompilerParams(vmem_limit_bytes=56 << 20),
    )(*results)


def solution(mesh):
    both = P(("dp", "mp"), None)
    return jax.shard_map(
        per_device,
        mesh=mesh,
        in_specs=(both, both, both, P("mp", "dp"), both, P(), P()),
        out_specs=(both, both, both),
        check_vma=False,
    )
```
